32 devices in a mesh: seq: 16 (over z, x, core), tp: 2 (over y).
Axes of the slice: x: 2, y: 2, z: 4, core: 2. Of those that a mesh axis runs over, the one named last changes fastest.
Arguments:
- trunk: bfloat16 [2048, 4096], P('seq', 'tp')
- trunk_gain: bfloat16 [4096], P('tp'), may hold values from 0.25 to 1.75
- w_in: bfloat16 [8, 1024, 4096], P('tp'), may hold values from -0.09375 to 0.09375
- depth_gain: bfloat16 [1024], replicated, may hold values from 0.25 to 1.75
- w_qkv: bfloat16 [8, 3072, 1024], P('tp', 'seq')
- w_out: bfloat16 [8, 1024, 1024], P('tp', 'seq'), may hold values from -0.1875 to 0.1875
- text_table: bfloat16 [16000, 1024], P(None, 'seq'), may hold values from -6 to 6
- audio_table: bfloat16 [7, 2048, 1024], P(None, None, 'seq'), may hold values from -6 to 6
- text_ids: int32 [2048], replicated, may hold values from 0 to 15999
- audio_ids: int32 [2048, 7], replicated, may hold values from 0 to 2047
- depth_cot: bfloat16 [8, 2048, 1024], P('tp', 'seq'), may hold values from -6 to 6
Outputs:
- depth_out: bfloat16 [8, 2048, 1024], P('tp', 'seq')
- trunk_grad: bfloat16 [2048, 4096], P('seq', 'tp')
- qkv_grad: float32 [8, 3072, 1024], P('tp', 'seq')
- out_grad: float32 [8, 1024, 1024], P('tp', 'seq')
The draws below stay inside these ranges and needn't reach their ends.
All inputs are finite; a program needn't handle non-finite values.
Results may differ from the reference program's by a relative error of at most 0.028.
The reference program's roundings to bfloat16 on the way count: a program that leaves them out, or rounds other values in their place, can miss the bound.
Values may be sent and summed in bfloat16 or wider, within the bound.
A program may use at most 192 MiB of HBM per device.

```python
import math
import jax
import jax.numpy as jnp
import numpy as np
from jax import lax

MODEL_DIM = 4096
DEPTH_DIM = 1024
HEADS = 16
HEAD_DIM = 64
CODEBOOKS = 8
CARD = 2048
TEXT_VOCAB = 16000
TOK_DEV = 128
TOKENS = 2048
N_SEQ = 16


def draw_trunk(key, part):
    first, second = jax.random.split(jax.random.fold_in(key, 11), 2)
    rows = jnp.exp(jax.random.uniform(second, (TOKENS, 1), jnp.float32, 0.0, math.log(10.0)))
    ramp = 1.0 + 2.0 * jnp.arange(MODEL_DIM, dtype=jnp.float32)[None, :] / MODEL_DIM
    base = jax.random.normal(first, (TOKENS, MODEL_DIM), jnp.float32)
    return (base * rows * ramp).astype(jnp.bfloat16)


def draw_w_qkv(key, part):
    base = jax.random.normal(jax.random.fold_in(key, 23), (CODEBOOKS, 3 * DEPTH_DIM, DEPTH_DIM), jnp.float32) / math.sqrt(DEPTH_DIM)
    return base.astype(jnp.bfloat16)


def with_ends(values, key, least, largest):
    place = [jax.random.randint(jax.random.fold_in(key, axis), (), 0, length) for axis, length in enumerate(values.shape)]
    main_axis = values.shape.index(max(values.shape))
    next_to = place[:main_axis] + [(place[main_axis] + 1) % values.shape[main_axis]] + place[main_axis + 1:]
    return values.at[tuple(place)].set(least).at[tuple(next_to)].set(largest)


def raised(entries, rng, source, target, blocks, factor):
    def block_of(position):
        return (jnp.arange(entries.shape[position]) // (entries.shape[position] // blocks)).reshape((-1,) + (1,) * (entries.ndim - 1 - position))

    near = jax.random.permutation(rng, blocks)[block_of(target)]
    second = (block_of(target) + blocks // 2) % blocks
    return jnp.where((block_of(source) == near) | (block_of(source) == second), factor * entries, entries)


def steps_of(own_key, shape, pieces, low, largest):
    factor_of = 1.0
    for position, blocks in pieces:
        draws = jax.random.uniform(jax.random.fold_in(jax.random.fold_in(own_key, 6), position), (blocks,), jnp.float32, low / len(pieces), largest / len(pieces))
        factor_of = factor_of * jnp.repeat(jnp.exp(draws), shape[position] // blocks).reshape((-1,) + (1,) * (len(shape) - 1 - position))
    return factor_of


def rank_bounds(count, slope):
    portions = [(1 << 20) // math.isqrt(rank ** slope) + 1 for rank in range(1, count + 1)]
    scale = 1 + sum(portions) // (1 << 30)
    return np.cumsum(np.array([max(1, weight // scale) for weight in portions]))


def skewed_ids(rng, dims, amount, skew):
    listing = rank_bounds(amount, skew)
    pick = jax.random.randint(jax.random.fold_in(rng, 1), dims, 0, int(listing[amount - 1]))
    rank = jnp.searchsorted(jnp.asarray(listing, jnp.int32), pick, side="right")
    return jax.random.permutation(jax.random.fold_in(rng, 2), amount)[rank].astype(jnp.int32)


def noise(rng, shape, spread, bound, cuts=(), kind=jnp.bfloat16):
    level = steps_of(rng, shape, cuts, -0.22, 0.18) if cuts else 1.0
    drawn = jax.random.normal(rng, shape, jnp.float32) * spread * level
    return jnp.minimum(jnp.maximum(drawn, -bound), bound).astype(kind)


def heavy_noise(stream_key, extent, deviation, bound, cuts, heavy, held_as=jnp.bfloat16):
    array = deviation * jax.random.normal(stream_key, extent, jnp.float32)
    if cuts:
        array = array * steps_of(stream_key, extent, cuts, -0.22, 0.18)
    return jnp.clip(raised(array, jax.random.fold_in(stream_key, 3), *heavy), -bound, bound).astype(held_as)


def setup_inputs(seed: int = 0) -> dict:
    seeds = jax.random.split(jax.random.key(seed), 12)
    trunk = draw_trunk(jax.random.fold_in(seeds[11], 71), 0)
    trunk_gain = jnp.clip(1.0 + 0.15 * jax.random.normal(seeds[1], (MODEL_DIM,), jnp.float32), 0.25, 1.75).astype(jnp.bfloat16)
    w_in = noise(seeds[2], (CODEBOOKS, DEPTH_DIM, MODEL_DIM), MODEL_DIM ** -0.5, 0.09375, ((0, 2),))
    depth_gain = jnp.clip(1.0 + 0.15 * jax.random.normal(seeds[3], (DEPTH_DIM,), jnp.float32), 0.25, 1.75).astype(jnp.bfloat16)
    w_qkv = draw_w_qkv(jax.random.fold_in(seeds[11], 71), 0)
    w_out = noise(seeds[5], (CODEBOOKS, DEPTH_DIM, DEPTH_DIM), DEPTH_DIM ** -0.5, 0.1875, ((0, 2), (1, 16)))
    text_table = noise(seeds[6], (TEXT_VOCAB, DEPTH_DIM), 1.0, 6.0, ((1, 16),))
    audio_table = noise(seeds[7], (CODEBOOKS - 1, CARD, DEPTH_DIM), 1.0, 6.0, ((2, 16),))
    text_ids = with_ends(skewed_ids(seeds[8], (TOKENS,), TEXT_VOCAB, 2), jax.random.fold_in(seeds[8], 3), 0, TEXT_VOCAB - 1).astype(jnp.int32)
    audio_ids = with_ends(skewed_ids(seeds[9], (TOKENS, CODEBOOKS - 1), CARD, 1), jax.random.fold_in(seeds[9], 3), 0, CARD - 1).astype(jnp.int32)
    depth_cot = heavy_noise(seeds[10], (CODEBOOKS, TOKENS, DEPTH_DIM), 1.0, 6.0, ((0, 2), (1, 16)), (1, 2, 16, 2.0))
    return {"trunk": trunk, "trunk_gain": trunk_gain, "w_in": w_in, "depth_gain": depth_gain, "w_qkv": w_qkv, "w_out": w_out, "text_table": text_table, "audio_table": audio_table, "text_ids": text_ids, "audio_ids": audio_ids, "depth_cot": depth_cot}


EPSILON = 1e-05

def inverse_rms(values):
    return lax.rsqrt(lax.optimization_barrier(jnp.mean(values * values, axis=-1, keepdims=True)) + EPSILON)

def causal_mask(count):
    order = jnp.arange(count)
    return order[:, None] >= order[None, :]

def softmax_rows(scores, count):
    masked = jnp.where(causal_mask(count), scores, -jnp.inf)
    highest = lax.optimization_barrier(jnp.max(masked, axis=-1, keepdims=True))
    shifted = jnp.exp(masked - highest)
    return shifted / lax.optimization_barrier(jnp.sum(shifted, axis=-1, keepdims=True))

def block_products(left, right):
    count = left.shape[0]
    left_blocks = jnp.moveaxis(left.reshape(count, N_SEQ, TOK_DEV, left.shape[2]), 1, 0)
    right_blocks = jnp.moveaxis(right.reshape(count, N_SEQ, TOK_DEV, right.shape[2]), 1, 0)

    def add_block(total, blocks):
        term = jnp.einsum('ctj,cti->cji', blocks[0].astype(jnp.float32), blocks[1].astype(jnp.float32))
        rounded = lax.optimization_barrier(term.astype(jnp.bfloat16))
        return (total + rounded.astype(jnp.float32), None)
    begin = jnp.zeros((count, left.shape[2], right.shape[2]), jnp.float32)
    total, unused = lax.scan(add_block, begin, (left_blocks, right_blocks))
    return total

def reference(trunk, trunk_gain, w_in, depth_gain, w_qkv, w_out, text_table, audio_table, text_ids, audio_ids, depth_cot):
    trunk_float = trunk.astype(jnp.float32)
    trunk_weight = trunk_gain.astype(jnp.float32)
    row_scale = inverse_rms(trunk_float)
    normed = (trunk_float * row_scale * trunk_weight).astype(jnp.bfloat16)
    text_rows = jnp.take(text_table, text_ids, axis=0)
    audio_rows = jax.vmap(lambda table, tokens: jnp.take(table, tokens, axis=0), in_axes=(0, 1))(audio_table, audio_ids)
    embedded = jnp.concatenate([text_rows[None], audio_rows], axis=0)

    def project_in(pair):
        return jnp.dot(normed, pair[0].T, preferred_element_type=jnp.float32) + pair[1].astype(jnp.float32)
    hidden = lax.map(project_in, (w_in, embedded))
    depth_scale = inverse_rms(hidden)
    depth_weight = depth_gain.astype(jnp.float32)
    depth_normed = (hidden * depth_scale * depth_weight).astype(jnp.bfloat16)
    projected = lax.map(lambda pair: jnp.dot(pair[0], pair[1].T, preferred_element_type=jnp.float32).astype(jnp.bfloat16), (depth_normed, w_qkv))
    parts = projected.reshape(CODEBOOKS, TOKENS, 3, HEADS, HEAD_DIM).astype(jnp.float32)
    query, keys, values = (parts[:, :, 0], parts[:, :, 1], parts[:, :, 2])
    root = math.sqrt(HEAD_DIM)
    scores = jnp.einsum('ithd,jthd->thij', query, keys) / root
    probs = softmax_rows(scores, CODEBOOKS)
    weights_low = probs.astype(jnp.bfloat16)
    attended = jnp.einsum('thij,jthd->ithd', weights_low.astype(jnp.float32), values).astype(jnp.bfloat16)
    attended = attended.reshape(CODEBOOKS, TOKENS, DEPTH_DIM)
    out_terms = lax.map(lambda pair: jnp.dot(pair[0], pair[1].T, preferred_element_type=jnp.float32), (attended, w_out))
    depth_out = (hidden + out_terms).astype(jnp.bfloat16)
    out_grad = block_products(depth_cot, attended)
    d_attended = lax.map(lambda pair: jnp.dot(pair[0], pair[1], preferred_element_type=jnp.float32).astype(jnp.bfloat16), (depth_cot, w_out))
    d_heads = d_attended.reshape(CODEBOOKS, TOKENS, HEADS, HEAD_DIM).astype(jnp.float32)
    d_weights = jnp.einsum('ithd,jthd->thij', d_heads, values)
    d_values = jnp.einsum('thij,ithd->jthd', weights_low.astype(jnp.float32), d_heads)
    d_scores = probs * (d_weights - lax.optimization_barrier(jnp.sum(probs * d_weights, axis=-1, keepdims=True)))
    d_query = jnp.einsum('thij,jthd->ithd', d_scores, keys) / root
    d_keys = jnp.einsum('thij,ithd->jthd', d_scores, query) / root
    d_projected = jnp.stack([d_query, d_keys, d_values], axis=2).astype(jnp.bfloat16)
    d_projected = d_projected.reshape(CODEBOOKS, TOKENS, 3 * DEPTH_DIM)
    qkv_grad = block_products(d_projected, depth_normed)
    d_normed = lax.map(lambda pair: jnp.dot(pair[0], pair[1], preferred_element_type=jnp.float32), (d_projected, w_qkv))
    gained = depth_weight * d_normed
    d_hidden = depth_cot.astype(jnp.float32) + depth_scale * gained
    d_hidden = d_hidden - hidden * depth_scale ** 3 * lax.optimization_barrier(jnp.mean(hidden * gained, axis=-1, keepdims=True))
    d_hidden = d_hidden.astype(jnp.bfloat16)

    def add_codebook(total, pair):
        return (total + jnp.dot(pair[0], pair[1], preferred_element_type=jnp.float32), None)
    d_features, unused = lax.scan(add_codebook, jnp.zeros((TOKENS, MODEL_DIM), jnp.float32), (d_hidden, w_in))
    trunk_gained = trunk_weight * d_features
    trunk_grad = row_scale * trunk_gained - trunk_float * row_scale ** 3 * lax.optimization_barrier(jnp.mean(trunk_float * trunk_gained, axis=-1, keepdims=True))
    return (depth_out, trunk_grad.astype(jnp.bfloat16), qkv_grad, out_grad)
```

```python
import math

import jax
import jax.numpy as jnp
from jax import lax
from jax.sharding import PartitionSpec as P

DEPTH_DIM = 1024
HEADS = 16
HEAD_DIM = 64


EPSILON = 1e-05


def inverse_rms(values):
    return lax.rsqrt(jnp.mean(values * values, axis=-1, keepdims=True) + EPSILON)


def causal_mask(count):
    order = jnp.arange(count)
    return order[:, None] >= order[None, :]


def softmax_rows(scores, count):
    masked = jnp.where(causal_mask(count), scores, -jnp.inf)
    highest = jnp.max(masked, axis=-1, keepdims=True)
    shifted = jnp.exp(masked - highest)
    return shifted / jnp.sum(shifted, axis=-1, keepdims=True)


def to_timesteps(values):
    return lax.all_to_all(values, "tp", split_axis=1, concat_axis=0, tiled=True)


def to_codebooks(values):
    return lax.all_to_all(values, "tp", split_axis=0, concat_axis=1, tiled=True)


def local(
    trunk,
    trunk_gain,
    w_in,
    depth_gain,
    w_qkv,
    w_out,
    text_table,
    audio_table,
    text_ids,
    audio_ids,
    depth_cot,
):
    model_width = trunk.shape[1] * lax.axis_size("tp")
    local_books = w_in.shape[0]
    trunk_float = trunk.astype(jnp.float32)
    gain_local = trunk_gain.astype(jnp.float32)
    whole_rows, whole_gain = (
        lax.all_gather(trunk, "tp", axis=1, tiled=True),
        lax.all_gather(trunk_gain.reshape(1, -1), "tp", axis=1, tiled=True),
    )
    whole_float = whole_rows.astype(jnp.float32)
    row_scale = inverse_rms(whole_float)
    normed = (whole_float * row_scale * whole_gain.astype(jnp.float32)).astype(jnp.bfloat16)
    first_book = lax.axis_index("tp") * local_books
    text_rows = jnp.take(text_table, text_ids, axis=0)
    columns = []
    for offset in range(local_books):
        book_index = first_book + offset
        earlier = jnp.maximum(book_index - 1, 0)
        table = lax.dynamic_index_in_dim(audio_table, earlier, 0, keepdims=False)
        tokens = lax.dynamic_index_in_dim(audio_ids, earlier, 1, keepdims=False)
        columns.append(jnp.where(book_index == 0, text_rows, jnp.take(table, tokens, axis=0)))
    embedded = lax.all_to_all(jnp.stack(columns), "seq", split_axis=1, concat_axis=2, tiled=True)
    hidden = jnp.einsum(
        "td,cjd->ctj", normed, w_in, preferred_element_type=jnp.float32
    ) + embedded.astype(jnp.float32)
    depth_scale = inverse_rms(hidden)
    depth_weight = depth_gain.astype(jnp.float32)
    depth_normed = (hidden * depth_scale * depth_weight).astype(jnp.bfloat16)
    qkv_full = lax.all_gather(w_qkv, "seq", axis=1, tiled=True)
    cot_here, depth_normed = lax.optimization_barrier((depth_cot, depth_normed))
    cot_columns = lax.all_to_all(cot_here, "seq", split_axis=2, concat_axis=1, tiled=True)
    cot_columns, depth_normed = lax.optimization_barrier((cot_columns, depth_normed))
    projected = jnp.einsum(
        "ctm,cjm->ctj", depth_normed, qkv_full, preferred_element_type=jnp.float32
    ).astype(jnp.bfloat16)
    w_out, projected = lax.optimization_barrier((w_out, projected))
    out_full = lax.all_gather(w_out, "seq", axis=1, tiled=True)
    d_attended = jnp.einsum(
        "ctj,cji->cti", depth_cot, out_full, preferred_element_type=jnp.float32
    ).astype(jnp.bfloat16)
    timed = to_timesteps(projected)
    rows_here, timed = lax.optimization_barrier((depth_normed, timed))
    normed_all = lax.all_gather(rows_here, "seq", axis=1, tiled=True)
    books, steps_here = (timed.shape[0], timed.shape[1])
    parts = timed.reshape(books, steps_here, 3, HEADS, HEAD_DIM)
    query, keys, values = (parts[:, :, 0], parts[:, :, 1], parts[:, :, 2])
    root = math.sqrt(HEAD_DIM)
    scores = jnp.einsum("ithd,jthd->thij", query, keys, preferred_element_type=jnp.float32) / root
    probs = softmax_rows(scores, books)
    weights_low = probs.astype(jnp.bfloat16)
    attended_time = jnp.einsum(
        "thij,jthd->ithd", weights_low, values, preferred_element_type=jnp.float32
    ).astype(jnp.bfloat16)
    attended = to_codebooks(attended_time.reshape(books, steps_here, DEPTH_DIM))
    out_terms = jnp.einsum("ctm,cjm->ctj", attended, out_full, preferred_element_type=jnp.float32)
    depth_out = (hidden + out_terms).astype(jnp.bfloat16)
    attended_all = lax.all_gather(attended, "seq", axis=1, tiled=True)
    out_grad = jnp.einsum(
        "ctj,cti->cji", cot_columns, attended_all, preferred_element_type=jnp.float32
    )
    d_time = to_timesteps(d_attended).reshape(books, steps_here, HEADS, HEAD_DIM)
    d_weights = jnp.einsum("ithd,jthd->thij", d_time, values, preferred_element_type=jnp.float32)
    d_values = jnp.einsum(
        "thij,ithd->jthd", weights_low, d_time, preferred_element_type=jnp.float32
    )
    d_scores = probs * (d_weights - jnp.sum(probs * d_weights, axis=-1, keepdims=True))
    d_query = jnp.einsum("thij,jthd->ithd", d_scores, keys.astype(jnp.float32)) / root
    d_keys = jnp.einsum("thij,ithd->jthd", d_scores, query.astype(jnp.float32)) / root
    d_joined = jnp.stack([d_query, d_keys, d_values], axis=2).astype(jnp.bfloat16)
    d_projected = to_codebooks(d_joined.reshape(books, steps_here, 3 * DEPTH_DIM))
    d_projected, normed_all = lax.optimization_barrier((d_projected, normed_all))
    d_columns = lax.all_to_all(d_projected, "seq", split_axis=2, concat_axis=1, tiled=True)
    qkv_grad = jnp.einsum(
        "ctj,cti->cji", d_columns, normed_all, preferred_element_type=jnp.float32
    )
    d_normed = jnp.einsum("ctj,cjm->ctm", d_projected, qkv_full, preferred_element_type=jnp.float32)
    gained = depth_weight * d_normed
    d_hidden = depth_cot.astype(jnp.float32) + depth_scale * gained
    d_hidden = d_hidden - hidden * depth_scale**3 * jnp.mean(
        hidden * gained, axis=-1, keepdims=True
    )
    d_hidden = d_hidden.astype(jnp.bfloat16)
    d_partial = jnp.einsum("ctj,cjd->td", d_hidden, w_in, preferred_element_type=jnp.float32)
    d_features = lax.psum_scatter(
        d_partial.astype(jnp.bfloat16), "tp", scatter_dimension=1, tiled=True
    ).astype(jnp.float32)
    trunk_gained = gain_local * d_features
    row_total = lax.psum(jnp.sum(trunk_float * trunk_gained, axis=1, keepdims=True), "tp")
    trunk_grad = row_scale * trunk_gained - trunk_float * row_scale**3 * row_total / model_width
    return (depth_out, trunk_grad.astype(jnp.bfloat16), qkv_grad, out_grad)


def solution(mesh):
    in_specs = (
        P("seq", "tp"),
        P("tp"),
        P("tp", None, None),
        P(),
        P("tp", "seq", None),
        P("tp", "seq", None),
        P(None, "seq"),
        P(None, None, "seq"),
        P(),
        P(),
        P("tp", "seq", None),
    )
    out_specs = (P("tp", "seq", None), P("seq", "tp"), P("tp", "seq", None), P("tp", "seq", None))
    return jax.shard_map(local, mesh=mesh, in_specs=in_specs, out_specs=out_specs, check_vma=False)
```

```python
import math

import jax
import jax.numpy as jnp
from jax import lax
from jax.sharding import PartitionSpec as P

DEPTH_DIM = 1024
HEADS = 16
HEAD_DIM = 64


EPSILON = 1e-05


def inverse_rms(values):
    return lax.rsqrt(jnp.mean(values * values, axis=-1, keepdims=True) + EPSILON)


def causal_mask(count):
    order = jnp.arange(count)
    return order[:, None] >= order[None, :]


def softmax_rows(scores, count):
    masked = jnp.where(causal_mask(count), scores, -jnp.inf)
    highest = jnp.max(masked, axis=-1, keepdims=True)
    shifted = jnp.exp(masked - highest)
    return shifted / jnp.sum(shifted, axis=-1, keepdims=True)


def to_timesteps(values):
    return lax.all_to_all(values, "tp", split_axis=1, concat_axis=0, tiled=True)


def to_codebooks(values):
    return lax.all_to_all(values, "tp", split_axis=0, concat_axis=1, tiled=True)


def local(
    trunk,
    trunk_gain,
    w_in,
    depth_gain,
    w_qkv,
    w_out,
    text_table,
    audio_table,
    text_ids,
    audio_ids,
    depth_cot,
):
    model_width = trunk.shape[1] * lax.axis_size("tp")
    local_books = w_in.shape[0]
    trunk_float = trunk.astype(jnp.float32)
    gain_local = trunk_gain.astype(jnp.float32)
    whole_rows, whole_gain = (
        lax.all_gather(trunk, "tp", axis=1, tiled=True),
        lax.all_gather(trunk_gain.reshape(1, -1), "tp", axis=1, tiled=True),
    )
    whole_float = whole_rows.astype(jnp.float32)
    row_scale = inverse_rms(whole_float)
    normed = (whole_float * row_scale * whole_gain.astype(jnp.float32)).astype(jnp.bfloat16)
    first_book = lax.axis_index("tp") * local_books
    text_rows = jnp.take(text_table, text_ids, axis=0)
    columns = []
    for offset in range(local_books):
        book_index = first_book + offset
        earlier = jnp.maximum(book_index - 1, 0)
        table = lax.dynamic_index_in_dim(audio_table, earlier, 0, keepdims=False)
        tokens = lax.dynamic_index_in_dim(audio_ids, earlier, 1, keepdims=False)
        columns.append(jnp.where(book_index == 0, text_rows, jnp.take(table, tokens, axis=0)))
    embedded = lax.all_to_all(jnp.stack(columns), "seq", split_axis=1, concat_axis=2, tiled=True)
    hidden = jnp.einsum(
        "td,cjd->ctj", normed, w_in, preferred_element_type=jnp.float32
    ) + embedded.astype(jnp.float32)
    depth_scale = inverse_rms(hidden)
    depth_weight = depth_gain.astype(jnp.float32)
    depth_normed = (hidden * depth_scale * depth_weight).astype(jnp.bfloat16)
    qkv_full = lax.all_gather(w_qkv, "seq", axis=1, tiled=True)
    projected = jnp.einsum(
        "ctm,cjm->ctj", depth_normed, qkv_full, preferred_element_type=jnp.float32
    ).astype(jnp.bfloat16)
    w_out, projected = lax.optimization_barrier((w_out, projected))
    out_full = lax.all_gather(w_out, "seq", axis=1, tiled=True)
    d_attended = jnp.einsum(
        "ctj,cji->cti", depth_cot, out_full, preferred_element_type=jnp.float32
    ).astype(jnp.bfloat16)
    timed = to_timesteps(projected)
    rows_here, timed = lax.optimization_barrier((depth_normed, timed))
    normed_all = lax.all_gather(rows_here, "seq", axis=1, tiled=True)
    books, steps_here = (timed.shape[0], timed.shape[1])
    parts = timed.reshape(books, steps_here, 3, HEADS, HEAD_DIM)
    query, keys, values = (parts[:, :, 0], parts[:, :, 1], parts[:, :, 2])
    root = math.sqrt(HEAD_DIM)
    scores = jnp.einsum("ithd,jthd->thij", query, keys, preferred_element_type=jnp.float32) / root
    probs = softmax_rows(scores, books)
    weights_low = probs.astype(jnp.bfloat16)
    attended_time = jnp.einsum(
        "thij,jthd->ithd", weights_low, values, preferred_element_type=jnp.float32
    ).astype(jnp.bfloat16)
    attended = to_codebooks(attended_time.reshape(books, steps_here, DEPTH_DIM))
    out_terms = jnp.einsum("ctm,cjm->ctj", attended, out_full, preferred_element_type=jnp.float32)
    depth_out = (hidden + out_terms).astype(jnp.bfloat16)
    indices = lax.axis_size("seq")
    near = 2 if indices % 2 == 0 else 1
    far = indices // near
    pairs = [[near * k + i for i in range(near)] for k in range(far)]
    strides = [[near * k + i for k in range(far)] for i in range(near)]
    cot_split = depth_cot.reshape(local_books, depth_cot.shape[1], far, near, -1)
    out_term = jnp.einsum(
        "ctfnj,cti->nfcji", cot_split, attended, preferred_element_type=jnp.float32
    ).astype(jnp.bfloat16)
    out_term = lax.all_to_all(
        out_term, "seq", split_axis=0, concat_axis=0, axis_index_groups=pairs, tiled=True
    )
    out_term = jnp.sum(out_term.astype(jnp.float32), axis=0).astype(jnp.bfloat16)
    out_sum = lax.psum_scatter(
        out_term, "seq", scatter_dimension=0, axis_index_groups=strides, tiled=False
    )
    d_time = to_timesteps(d_attended).reshape(books, steps_here, HEADS, HEAD_DIM)
    d_weights = jnp.einsum("ithd,jthd->thij", d_time, values, preferred_element_type=jnp.float32)
    d_values = jnp.einsum(
        "thij,ithd->jthd", weights_low, d_time, preferred_element_type=jnp.float32
    )
    d_scores = probs * (d_weights - jnp.sum(probs * d_weights, axis=-1, keepdims=True))
    d_query = jnp.einsum("thij,jthd->ithd", d_scores, keys.astype(jnp.float32)) / root
    d_keys = jnp.einsum("thij,ithd->jthd", d_scores, query.astype(jnp.float32)) / root
    d_joined = jnp.stack([d_query, d_keys, d_values], axis=2).astype(jnp.bfloat16)
    d_projected = to_codebooks(d_joined.reshape(books, steps_here, 3 * DEPTH_DIM))
    d_projected, normed_all = lax.optimization_barrier((d_projected, normed_all))
    d_columns = lax.all_to_all(d_projected, "seq", split_axis=2, concat_axis=1, tiled=True)
    qkv_grad = jnp.einsum(
        "ctj,cti->cji", d_columns, normed_all, preferred_element_type=jnp.float32
    )
    d_normed = jnp.einsum("ctj,cjm->ctm", d_projected, qkv_full, preferred_element_type=jnp.float32)
    gained = depth_weight * d_normed
    d_hidden = depth_cot.astype(jnp.float32) + depth_scale * gained
    d_hidden = d_hidden - hidden * depth_scale**3 * jnp.mean(
        hidden * gained, axis=-1, keepdims=True
    )
    d_hidden = d_hidden.astype(jnp.bfloat16)
    d_partial = jnp.einsum("ctj,cjd->td", d_hidden, w_in, preferred_element_type=jnp.float32)
    sides = lax.axis_size("tp")
    d_pieces = d_partial.astype(jnp.bfloat16).reshape(trunk.shape[0], sides, -1)
    d_pieces = lax.all_to_all(d_pieces, "tp", split_axis=1, concat_axis=1, tiled=True)
    d_features = jnp.sum(d_pieces.astype(jnp.float32), axis=1)
    trunk_gained = gain_local * d_features
    row_total = lax.psum(jnp.sum(trunk_float * trunk_gained, axis=1, keepdims=True), "tp")
    trunk_grad = row_scale * trunk_gained - trunk_float * row_scale**3 * row_total / model_width
    trunk_grad = trunk_grad.astype(jnp.bfloat16)
    out_sum, trunk_grad, qkv_grad = lax.optimization_barrier((out_sum, trunk_grad, qkv_grad))
    out_grad = out_sum.astype(jnp.float32)
    return (depth_out, trunk_grad, qkv_grad, out_grad)


def solution(mesh):
    in_specs = (
        P("seq", "tp"),
        P("tp"),
        P("tp", None, None),
        P(),
        P("tp", "seq", None),
        P("tp", "seq", None),
        P(None, "seq"),
        P(None, None, "seq"),
        P(),
        P(),
        P("tp", "seq", None),
    )
    out_specs = (P("tp", "seq", None), P("seq", "tp"), P("tp", "seq", None), P("tp", "seq", None))
    return jax.shard_map(local, mesh=mesh, in_specs=in_specs, out_specs=out_specs, check_vma=False)
```

```python
import math

import jax
import jax.numpy as jnp
from jax import lax
from jax.sharding import PartitionSpec as P

DEPTH_DIM = 1024
HEADS = 16
HEAD_DIM = 64


EPSILON = 1e-05


def inverse_rms(values):
    return lax.rsqrt(jnp.mean(values * values, axis=-1, keepdims=True) + EPSILON)


def causal_mask(count):
    order = jnp.arange(count)
    return order[:, None] >= order[None, :]


def softmax_rows(scores, count):
    masked = jnp.where(causal_mask(count), scores, -jnp.inf)
    highest = jnp.max(masked, axis=-1, keepdims=True)
    shifted = jnp.exp(masked - highest)
    return shifted / jnp.sum(shifted, axis=-1, keepdims=True)


def to_timesteps(values):
    return lax.all_to_all(values, "tp", split_axis=1, concat_axis=0, tiled=True)


def to_codebooks(values):
    return lax.all_to_all(values, "tp", split_axis=0, concat_axis=1, tiled=True)


def local(
    trunk,
    trunk_gain,
    w_in,
    depth_gain,
    w_qkv,
    w_out,
    text_table,
    audio_table,
    text_ids,
    audio_ids,
    depth_cot,
):
    model_width = trunk.shape[1] * lax.axis_size("tp")
    local_books = w_in.shape[0]
    trunk_float = trunk.astype(jnp.float32)
    gain_local = trunk_gain.astype(jnp.float32)
    whole_rows, whole_gain = (
        lax.all_gather(trunk, "tp", axis=1, tiled=True),
        lax.all_gather(trunk_gain.reshape(1, -1), "tp", axis=1, tiled=True),
    )
    whole_float = whole_rows.astype(jnp.float32)
    row_scale = inverse_rms(whole_float)
    normed = (whole_float * row_scale * whole_gain.astype(jnp.float32)).astype(jnp.bfloat16)
    first_book = lax.axis_index("tp") * local_books
    text_rows = jnp.take(text_table, text_ids, axis=0)
    columns = []
    for offset in range(local_books):
        book_index = first_book + offset
        earlier = jnp.maximum(book_index - 1, 0)
        table = lax.dynamic_index_in_dim(audio_table, earlier, 0, keepdims=False)
        tokens = lax.dynamic_index_in_dim(audio_ids, earlier, 1, keepdims=False)
        columns.append(jnp.where(book_index == 0, text_rows, jnp.take(table, tokens, axis=0)))
    embedded = lax.all_to_all(jnp.stack(columns), "seq", split_axis=1, concat_axis=2, tiled=True)
    hidden = jnp.einsum(
        "td,cjd->ctj", normed, w_in, preferred_element_type=jnp.float32
    ) + embedded.astype(jnp.float32)
    depth_scale = inverse_rms(hidden)
    depth_weight = depth_gain.astype(jnp.float32)
    depth_normed = (hidden * depth_scale * depth_weight).astype(jnp.bfloat16)
    qkv_full = lax.all_gather(w_qkv, "seq", axis=1, tiled=True)
    cot_here, depth_normed = lax.optimization_barrier((depth_cot, depth_normed))
    cot_columns = lax.all_to_all(cot_here, "seq", split_axis=2, concat_axis=1, tiled=True)
    cot_columns, depth_normed = lax.optimization_barrier((cot_columns, depth_normed))
    projected = jnp.einsum(
        "ctm,cjm->ctj", depth_normed, qkv_full, preferred_element_type=jnp.float32
    ).astype(jnp.bfloat16)
    w_out, projected = lax.optimization_barrier((w_out, projected))
    out_full = lax.all_gather(w_out, "seq", axis=1, tiled=True)
    d_attended = jnp.einsum(
        "ctj,cji->cti", depth_cot, out_full, preferred_element_type=jnp.float32
    ).astype(jnp.bfloat16)
    timed = to_timesteps(projected)
    rows_here, timed = lax.optimization_barrier((depth_normed, timed))
    normed_all = lax.all_gather(rows_here, "seq", axis=1, tiled=True)
    books, steps_here = (timed.shape[0], timed.shape[1])
    parts = timed.reshape(books, steps_here, 3, HEADS, HEAD_DIM)
    query, keys, values = (parts[:, :, 0], parts[:, :, 1], parts[:, :, 2])
    root = math.sqrt(HEAD_DIM)
    scores = jnp.einsum("ithd,jthd->thij", query, keys, preferred_element_type=jnp.float32) / root
    probs = softmax_rows(scores, books)
    weights_low = probs.astype(jnp.bfloat16)
    attended_time = jnp.einsum(
        "thij,jthd->ithd", weights_low, values, preferred_element_type=jnp.float32
    ).astype(jnp.bfloat16)
    attended = to_codebooks(attended_time.reshape(books, steps_here, DEPTH_DIM))
    out_terms = jnp.einsum("ctm,cjm->ctj", attended, out_full, preferred_element_type=jnp.float32)
    depth_out = (hidden + out_terms).astype(jnp.bfloat16)
    attended_all = lax.all_gather(attended, "seq", axis=1, tiled=True)
    d_time = to_timesteps(d_attended).reshape(books, steps_here, HEADS, HEAD_DIM)
    d_weights = jnp.einsum("ithd,jthd->thij", d_time, values, preferred_element_type=jnp.float32)
    d_values = jnp.einsum(
        "thij,ithd->jthd", weights_low, d_time, preferred_element_type=jnp.float32
    )
    d_scores = probs * (d_weights - jnp.sum(probs * d_weights, axis=-1, keepdims=True))
    d_query = jnp.einsum("thij,jthd->ithd", d_scores, keys.astype(jnp.float32)) / root
    d_keys = jnp.einsum("thij,ithd->jthd", d_scores, query.astype(jnp.float32)) / root
    d_joined = jnp.stack([d_query, d_keys, d_values], axis=2).astype(jnp.bfloat16)
    d_projected = to_codebooks(d_joined.reshape(books, steps_here, 3 * DEPTH_DIM))
    d_projected, normed_all = lax.optimization_barrier((d_projected, normed_all))
    d_columns = lax.all_to_all(d_projected, "seq", split_axis=2, concat_axis=1, tiled=True)
    qkv_grad = jnp.einsum(
        "ctj,cti->cji", d_columns, normed_all, preferred_element_type=jnp.float32
    )
    d_normed = jnp.einsum("ctj,cjm->ctm", d_projected, qkv_full, preferred_element_type=jnp.float32)
    gained = depth_weight * d_normed
    d_hidden = depth_cot.astype(jnp.float32) + depth_scale * gained
    d_hidden = d_hidden - hidden * depth_scale**3 * jnp.mean(
        hidden * gained, axis=-1, keepdims=True
    )
    d_hidden = d_hidden.astype(jnp.bfloat16)
    d_partial = jnp.einsum("ctj,cjd->td", d_hidden, w_in, preferred_element_type=jnp.float32)
    sides = lax.axis_size("tp")
    d_pieces = d_partial.astype(jnp.bfloat16).reshape(trunk.shape[0], sides, -1)
    d_pieces = lax.all_to_all(d_pieces, "tp", split_axis=1, concat_axis=1, tiled=True)
    d_features = jnp.sum(d_pieces.astype(jnp.float32), axis=1)
    trunk_gained = gain_local * d_features
    row_total = lax.psum(jnp.sum(trunk_float * trunk_gained, axis=1, keepdims=True), "tp")
    trunk_grad = row_scale * trunk_gained - trunk_float * row_scale**3 * row_total / model_width
    trunk_grad = trunk_grad.astype(jnp.bfloat16)
    attended_all, trunk_grad, qkv_grad = lax.optimization_barrier(
        (attended_all, trunk_grad, qkv_grad)
    )
    out_grad = jnp.einsum(
        "ctj,cti->cji", cot_columns, attended_all, preferred_element_type=jnp.float32
    )
    return (depth_out, trunk_grad, qkv_grad, out_grad)


def solution(mesh):
    in_specs = (
        P("seq", "tp"),
        P("tp"),
        P("tp", None, None),
        P(),
        P("tp", "seq", None),
        P("tp", "seq", None),
        P(None, "seq"),
        P(None, None, "seq"),
        P(),
        P(),
        P("tp", "seq", None),
    )
    out_specs = (P("tp", "seq", None), P("seq", "tp"), P("tp", "seq", None), P("tp", "seq", None))
    return jax.shard_map(local, mesh=mesh, in_specs=in_specs, out_specs=out_specs, check_vma=False)
```
